128 devices in a mesh: seq: 16 (over x, z_hi, core), ch: 8 (over z_lo, y).
Axes of the slice: x: 4, y: 4, z: 4 (z_hi: 2, z_lo: 2; z = z_hi * 2 + z_lo), core: 2. Of those that a mesh axis runs over, the one named last changes fastest.
Arguments:
- inputs: bfloat16 [1536, 131072], P('ch', 'seq'), may hold values from -6 to 6
- gating: bfloat16 [1536, 131072], P('ch', 'seq'), may hold values from -6 to 6
- upstream: bfloat16 [1536, 131072], P('ch', 'seq'), may hold values from -6 to 6
- factor_one: bfloat16 [512, 512], replicated, may hold values from -0.25 to 0.25
- factor_two: bfloat16 [256, 256], replicated, may hold values from -0.375 to 0.375
- factor_three: bfloat16 [256, 256], replicated, may hold values from -0.375 to 0.375
- factor_four: bfloat16 [512, 512], replicated, may hold values from -0.25 to 0.25
- kernel_cols: float32 [1536, 512], P('ch'), may hold values from -4 to 4
- kernel_rows: float32 [1536, 256], P('ch'), may hold values from -4 to 4
Outputs:
- input_grad: bfloat16 [1536, 131072], P('ch', 'seq')
- gating_grad: bfloat16 [1536, 131072], P('ch', 'seq')
- one_grad: float32 [512, 512], replicated
- two_grad: float32 [256, 256], replicated
- three_grad: float32 [256, 256], replicated
- four_grad: float32 [512, 512], replicated
- cols_grad: float32 [1536, 512], P('ch')
- rows_grad: float32 [1536, 256], P('ch')
The draws below stay inside these ranges and needn't reach their ends.
All inputs are finite; a program needn't handle non-finite values.
Results may differ from the reference program's by a relative error of at most 0.0076.
Values may be sent and summed in bfloat16 or wider, within the bound.
No kernel may reach another device: no remote copies, remote signals or barrier semaphores. Data moves between devices by JAX's collectives and lax.ppermute only.
A program may use at most 128 MiB of HBM per device.

```python
import math
import jax
import jax.numpy as jnp
from jax import lax

P1 = 256
P2 = 512
C = 1536
TOKENS = 131072


def block_levels(key, shape, cuts, low, largest):
    def one(dim, shards_of):
        draws = jax.random.uniform(jax.random.fold_in(jax.random.fold_in(key, 6), dim), (shards_of,), jnp.float32, low / len(cuts), largest / len(cuts))
        return jnp.repeat(jnp.exp(draws), shape[dim] // shards_of).reshape((-1,) + (1,) * (len(shape) - dim - 1))

    factor_of = one(*cuts[0])
    for cut in cuts[1:]:
        factor_of = factor_of * one(*cut)
    return factor_of


def bell_draw(stream_key, extent, scale, most, split=(), dtype=jnp.bfloat16):
    result = scale * jax.random.normal(stream_key, extent, jnp.float32)
    if split:
        result = result * block_levels(stream_key, extent, split, -0.22, 0.18)
    return jnp.clip(result, -most, most).astype(dtype)


def setup_inputs(seed: int = 0) -> dict:
    streams_of = jax.random.split(jax.random.key(seed), 10)
    inputs = bell_draw(streams_of[0], (C, TOKENS), 1.0, 6.0, ((0, 8), (1, 16)))
    gating = bell_draw(streams_of[1], (C, TOKENS), 1.0, 6.0, ((0, 8), (1, 16)))
    upstream = bell_draw(streams_of[2], (C, TOKENS), 1.0, 6.0, ((0, 8), (1, 16)))
    factor_one = bell_draw(streams_of[3], (P2, P2), P2 ** -0.5, 0.25)
    factor_two = bell_draw(streams_of[4], (P1, P1), P1 ** -0.5, 0.375)
    factor_three = bell_draw(streams_of[5], (P1, P1), P1 ** -0.5, 0.375)
    factor_four = bell_draw(streams_of[6], (P2, P2), P2 ** -0.5, 0.25)
    kernel_cols = bell_draw(streams_of[7], (C, P2), 1.0, 4.0, ((0, 8),), jnp.float32)
    kernel_rows = bell_draw(streams_of[8], (C, P1), 1.0, 4.0, ((0, 8),), jnp.float32)
    return dict(inputs=inputs, gating=gating, upstream=upstream, factor_one=factor_one, factor_two=factor_two, factor_three=factor_three, factor_four=factor_four, kernel_cols=kernel_cols, kernel_rows=kernel_rows)


def mult(form, left, right):
    return jnp.einsum(form, left.astype(jnp.float32), right.astype(jnp.float32), precision=lax.Precision.HIGHEST)

def reference(inputs, gating, upstream, factor_one, factor_two, factor_three, factor_four, kernel_cols, kernel_rows):
    width = math.gcd(C, 64)
    groups = C // width

    def one_group(packed):
        shaped, gate_rows, cotangent, kc, kr = packed
        first_prod = mult('cij,jk->cik', shaped, factor_one)
        first_out = (first_prod * kc[:, None, :]).astype(jnp.bfloat16)
        left_prod = mult('ki,cij->ckj', factor_two, first_out)
        left_out = (left_prod * kr[:, :, None]).astype(jnp.bfloat16)
        second = mult('ki,cij->ckj', factor_three, left_out).astype(jnp.bfloat16)
        final_prod = mult('cij,jk->cik', second, factor_four)
        gate_grad = (cotangent.astype(jnp.float32) * final_prod).astype(jnp.bfloat16)
        up_gate = (cotangent.astype(jnp.float32) * gate_rows.astype(jnp.float32)).astype(jnp.bfloat16)
        grad_four = mult('cij,cik->jk', second, up_gate)
        grad_second = mult('cik,jk->cij', up_gate, factor_four).astype(jnp.bfloat16)
        grad_three = mult('ckj,cij->ki', grad_second, left_out)
        grad_left = mult('ki,ckj->cij', factor_three, grad_second)
        rows_part = lax.optimization_barrier(jnp.sum(grad_left * left_prod, axis=2))
        grad_prod = (grad_left * kr[:, :, None]).astype(jnp.bfloat16)
        grad_two = mult('ckj,cij->ki', grad_prod, first_out)
        grad_first = mult('ki,ckj->cij', factor_two, grad_prod).astype(jnp.bfloat16)
        cols_part = lax.optimization_barrier(jnp.sum(grad_first.astype(jnp.float32) * first_prod, axis=1))
        grad_inner = (grad_first.astype(jnp.float32) * kc[:, None, :]).astype(jnp.bfloat16)
        grad_one = mult('cij,cik->jk', shaped, grad_inner)
        input_part = mult('cik,jk->cij', grad_inner, factor_one).astype(jnp.bfloat16)
        return (input_part, gate_grad, grad_one, grad_two, grad_three, grad_four, cols_part, rows_part)
    packed = (inputs.reshape(groups, width, P1, P2), gating.reshape(groups, width, P1, P2), upstream.reshape(groups, width, P1, P2), kernel_cols.reshape(groups, width, P2), kernel_rows.reshape(groups, width, P1))
    results = lax.map(one_group, packed)
    scale_one = 1.0 / math.sqrt(P1 * C)
    scale_two = 1.0 / math.sqrt(P2 * C)
    input_grad = results[0].reshape(C, TOKENS)
    gating_grad = results[1].reshape(C, TOKENS)
    one_grad = lax.optimization_barrier(jnp.sum(results[2], axis=0)) * scale_one
    two_grad = lax.optimization_barrier(jnp.sum(results[3], axis=0)) * scale_two
    three_grad = lax.optimization_barrier(jnp.sum(results[4], axis=0)) * scale_two
    four_grad = lax.optimization_barrier(jnp.sum(results[5], axis=0)) * scale_one
    cols_grad = results[6].reshape(C, P2) / math.sqrt(P1)
    rows_grad = results[7].reshape(C, P1) / math.sqrt(P2)
    return (input_grad, gating_grad, one_grad, two_grad, three_grad, four_grad, cols_grad, rows_grad)
```

```python
import math

import jax
import jax.numpy as jnp
from jax import lax
from jax.experimental import pallas as pl
from jax.experimental.pallas import tpu as pltpu
from jax.sharding import PartitionSpec as P

P1 = 256
P2 = 512
C = 1536
N_SEQ = 16
N_CH = 8
WIDTH = C // N_CH
OWNED = WIDTH // N_SEQ
ROWS = P1 // N_SEQ
LENGTH = ROWS * P2
BLOCK = 16
STEPS = WIDTH // BLOCK
PIECES = 8
HIGH_ONE = P2 // PIECES
HIGH_TWO = P1 // PIECES
PIECE_ROWS = 2 * HIGH_ONE + HIGH_TWO
AXES = ("seq", "ch")

flt = jnp.float32
half = jnp.bfloat16


def params():
    return pltpu.CompilerParams(vmem_limit_bytes=56 * 1024 * 1024)


def cost(flops, moved):
    return pl.CostEstimate(flops=int(flops), bytes_accessed=int(moved), transcendentals=0)


def nn(a, b):
    return lax.dot_general(a, b, (((1,), (0,)), ((), ())), preferred_element_type=flt)


def nt(a, b):
    return lax.dot_general(a, b, (((1,), (1,)), ((), ())), preferred_element_type=flt)


def tn(a, b):
    return lax.dot_general(a, b, (((0,), (0,)), ((), ())), preferred_element_type=flt)


def split_kernel(x_ref, out_ref):
    out_ref[...] = x_ref[...].reshape(out_ref.shape)


def gate_kernel(g_ref, z_ref, out_ref):
    prod = (g_ref[...].astype(flt) * z_ref[...].astype(flt)).astype(half)
    out_ref[...] = prod.reshape(out_ref.shape)


def join_kernel(x_ref, out_ref):
    out_ref[...] = x_ref[...].reshape(out_ref.shape)


def final_kernel(h_ref, g_ref, four_ref, out_ref):
    prod = nn(h_ref[...].reshape(BLOCK * ROWS, P2), four_ref[...])
    prod = prod.reshape(BLOCK, LENGTH)
    out_ref[...] = (g_ref[...].astype(flt) * prod).astype(half)


FLAT = pl.BlockSpec((BLOCK, LENGTH), lambda i: (i, 0))
MATS = pl.BlockSpec((BLOCK, ROWS, P2), lambda i: (i, 0, 0))
FLAT_SHAPE = jax.ShapeDtypeStruct((WIDTH, LENGTH), half)
MATS_SHAPE = jax.ShapeDtypeStruct((WIDTH, ROWS, P2), half)
SIZE = WIDTH * LENGTH * 2


def split(x):
    return pl.pallas_call(
        split_kernel, grid=(STEPS,), in_specs=[FLAT], out_specs=MATS, out_shape=MATS_SHAPE,
        compiler_params=params(), cost_estimate=cost(0, 2 * SIZE), name="split_rows",
    )(x)


def gate(g, z):
    return pl.pallas_call(
        gate_kernel, grid=(STEPS,), in_specs=[FLAT, FLAT], out_specs=MATS, out_shape=MATS_SHAPE,
        compiler_params=params(), cost_estimate=cost(0, 3 * SIZE), name="gate_rows",
    )(g, z)


def join(x):
    return pl.pallas_call(
        join_kernel, grid=(STEPS,), in_specs=[MATS], out_specs=FLAT, out_shape=FLAT_SHAPE,
        compiler_params=params(), cost_estimate=cost(0, 2 * SIZE), name="join_rows",
    )(x)


def final(h, g, four):
    return pl.pallas_call(
        final_kernel, grid=(STEPS,),
        in_specs=[MATS, FLAT, pl.BlockSpec((P2, P2), lambda i: (0, 0))],
        out_specs=FLAT, out_shape=FLAT_SHAPE, compiler_params=params(),
        cost_estimate=cost(2 * WIDTH * LENGTH * P2, 3 * SIZE), name="final_rows",
    )(h, g, four)


def forward_kernel(x_ref, one_ref, two_ref, three_ref, kc_ref, kr_ref, h_ref):
    x = x_ref[...].reshape(P1, P2)
    first = (nn(x, one_ref[...]) * kc_ref[0]).astype(half)
    left = (nn(two_ref[...], first) * kr_ref[0]).astype(half)
    second = nn(three_ref[...], left).astype(half)
    h_ref[...] = second.reshape(h_ref.shape)


def backward_kernel(
    x_ref, e_ref, one_ref, two_ref, three_ref, four_ref, two_t_ref, three_t_ref, kc_ref, kr_ref,
    dx_ref, cols_ref, rows_ref, grads_ref, acc_one, acc_two, acc_three, acc_four,
):
    step = pl.program_id(0)
    kc = kc_ref[0]
    kr = kr_ref[0]
    x = x_ref[...].reshape(P1, P2)
    e = e_ref[...].reshape(P1, P2)
    first_prod = nn(x, one_ref[...])
    first = (first_prod * kc).astype(half)
    left_prod = nn(two_ref[...], first)
    left = (left_prod * kr).astype(half)
    second = nn(three_ref[...], left).astype(half)
    d_second = nt(e, four_ref[...]).astype(half)
    d_left = nn(three_t_ref[...], d_second)
    rows_ref[0] = jnp.sum(d_left * left_prod, axis=1, keepdims=True)
    d_prod = (d_left * kr).astype(half)
    d_first = nn(two_t_ref[...], d_prod).astype(half).astype(flt)
    cols_ref[0] = jnp.sum(d_first * first_prod, axis=0, keepdims=True)
    d_inner = (d_first * kc).astype(half)
    dx_ref[...] = nt(d_inner, one_ref[...]).astype(half).reshape(dx_ref.shape)

    @pl.when(step == 0)
    def _():
        acc_one[...] = jnp.zeros_like(acc_one)
        acc_two[...] = jnp.zeros_like(acc_two)
        acc_three[...] = jnp.zeros_like(acc_three)
        acc_four[...] = jnp.zeros_like(acc_four)

    acc_four[...] += tn(second, e)
    acc_three[...] += nt(d_second, left)
    acc_two[...] += nt(d_prod, first)
    acc_one[...] += tn(x, d_inner)

    @pl.when(step == OWNED - 1)
    def _():
        for p in range(PIECES):
            wide = slice(p * HIGH_ONE, (p + 1) * HIGH_ONE)
            tall = slice(p * HIGH_TWO, (p + 1) * HIGH_TWO)
            grads_ref[p, 0:HIGH_ONE, :] = acc_one[wide, :]
            grads_ref[p, HIGH_ONE : HIGH_ONE + HIGH_TWO, 0:P1] = acc_two[tall, :]
            grads_ref[p, HIGH_ONE : HIGH_ONE + HIGH_TWO, P1 : 2 * P1] = acc_three[tall, :]
            grads_ref[p, HIGH_ONE + HIGH_TWO : PIECE_ROWS, :] = acc_four[wide, :]


def whole(*shape):
    return pl.BlockSpec(shape, lambda q: (0,) * len(shape))


OWN = pl.BlockSpec((N_SEQ, 1, ROWS, P2), lambda q: (0, q, 0, 0))
OWN_SHAPE = jax.ShapeDtypeStruct((N_SEQ, OWNED, ROWS, P2), half)
COL = pl.BlockSpec((1, 1, P2), lambda q: (q, 0, 0))
ROW = pl.BlockSpec((1, P1, 1), lambda q: (q, 0, 0))
BIG = 2 * P1 * P2 * P2 * OWNED
SMALL = 2 * P1 * P1 * P2 * OWNED


def forward(x, one, two, three, kc, kr):
    return pl.pallas_call(
        forward_kernel, grid=(OWNED,),
        in_specs=[OWN, whole(P2, P2), whole(P1, P1), whole(P1, P1), COL, ROW],
        out_specs=OWN, out_shape=OWN_SHAPE, compiler_params=params(),
        cost_estimate=cost(BIG + 2 * SMALL, 2 * SIZE), name="forward_owned",
    )(x, one, two, three, kc, kr)


def backward(x, e, one, two, three, four, two_t, three_t, kc, kr):
    return pl.pallas_call(
        backward_kernel, grid=(OWNED,),
        in_specs=[
            OWN, OWN, whole(P2, P2), whole(P1, P1), whole(P1, P1), whole(P2, P2),
            whole(P1, P1), whole(P1, P1), COL, ROW,
        ],
        out_specs=[OWN, COL, ROW, whole(PIECES, PIECE_ROWS, P2)],
        out_shape=[
            OWN_SHAPE,
            jax.ShapeDtypeStruct((OWNED, 1, P2), flt),
            jax.ShapeDtypeStruct((OWNED, P1, 1), flt),
            jax.ShapeDtypeStruct((PIECES, PIECE_ROWS, P2), flt),
        ],
        scratch_shapes=[
            pltpu.VMEM((P2, P2), flt), pltpu.VMEM((P1, P1), flt),
            pltpu.VMEM((P1, P1), flt), pltpu.VMEM((P2, P2), flt),
        ],
        compiler_params=params(),
        cost_estimate=cost(5 * BIG + 6 * SMALL, 3 * SIZE), name="backward_owned",
    )(x, e, one, two, three, four, two_t, three_t, kc, kr)


def swap_pairs(x=0, zh=0, core=0, zl=0, y=0):
    flip_seq = x * 4 + zh * 2 + core
    flip_ch = zl * 4 + y
    return [
        (s * N_CH + c, (s ^ flip_seq) * N_CH + (c ^ flip_ch))
        for s in range(N_SEQ)
        for c in range(N_CH)
    ]


def swap(v, **flips):
    return lax.ppermute(v, AXES, swap_pairs(**flips))


def pick(v, index):
    return lax.dynamic_index_in_dim(v, index, 0, keepdims=False)


def in_order(bit, mine, theirs):
    return jnp.where(bit == 0, jnp.stack([mine, theirs]), jnp.stack([theirs, mine]))


def four_in_order(place, own, near, far, other):
    low = in_order(place & 1, own, near)
    high = in_order(place & 1, far, other)
    return in_order(place >> 1, low, high).reshape(4, *own.shape)


def sum_over_four(v, axes):
    v = v.astype(half)
    one, two, three = (swap(v, **flips) for flips in axes)
    return (v.astype(flt) + one.astype(flt)) + (two.astype(flt) + three.astype(flt))


def reduce_grads(grads, core, y):
    parts = grads.reshape(2, 4, PIECE_ROWS, P2)
    kept = pick(parts, core) + swap(pick(parts, 1 - core).astype(half), core=1).astype(flt)
    got = [swap(pick(kept, y ^ d).astype(half), y=d).astype(flt) for d in (1, 2, 3)]
    mine = pick(kept, y) + got[0] + got[1] + got[2]
    mine = sum_over_four(mine, [dict(x=1), dict(x=2), dict(x=3)])
    mine = sum_over_four(mine, [dict(zl=1), dict(zh=1), dict(zh=1, zl=1)]).astype(half)
    near, far, other = (swap(mine, y=d) for d in (1, 2, 3))
    mine = four_in_order(y, mine, near, far, other)
    both = in_order(core, mine, swap(mine, core=1))
    return both.reshape(PIECES, PIECE_ROWS, P2).astype(flt)


def gather_owned(v, x, zh, core):
    v = in_order(core, v, swap(v, core=1))
    v = in_order(zh, v, swap(v, zh=1))
    near, far, other = (swap(v, x=d) for d in (1, 2, 3))
    return four_in_order(x, v, near, far, other).reshape(WIDTH, P1 + P2)


def exchange(v):
    return lax.all_to_all(v, "seq", split_axis=0, concat_axis=0, tiled=True)


def local(
    inputs,
    gating,
    upstream,
    factor_one,
    factor_two,
    factor_three,
    factor_four,
    kernel_cols,
    kernel_rows,
):
    seq = lax.axis_index("seq")
    ch = lax.axis_index("ch")
    x_at, zh_at, core_at, y_at = seq >> 2, (seq >> 1) & 1, seq & 1, ch & 3
    owned = (N_SEQ, OWNED, ROWS, P2)
    kc = lax.dynamic_slice_in_dim(kernel_cols, seq * OWNED, OWNED, 0).reshape(OWNED, 1, P2)
    kr = lax.dynamic_slice_in_dim(kernel_rows, seq * OWNED, OWNED, 0).reshape(OWNED, P1, 1)

    x_own = exchange(split(inputs)).reshape(owned)
    e_own = exchange(gate(upstream, gating)).reshape(owned)
    h_own = forward(x_own, factor_one, factor_two, factor_three, kc, kr)
    h_rows = exchange(h_own.reshape(WIDTH, ROWS, P2))
    dx_own, cols, rows, grads = backward(
        x_own, e_own, factor_one, factor_two, factor_three, factor_four,
        factor_two.T, factor_three.T, kc, kr,
    )
    dx_rows = exchange(dx_own.reshape(WIDTH, ROWS, P2))
    gating_grad = final(h_rows, upstream, factor_four)
    input_grad = join(dx_rows)

    total = reduce_grads(grads, core_at, y_at)
    scale_one = 1.0 / math.sqrt(P1 * C)
    scale_two = 1.0 / math.sqrt(P2 * C)
    one_grad = total[:, 0:HIGH_ONE, :].reshape(P2, P2) * scale_one
    mid = total[:, HIGH_ONE : HIGH_ONE + HIGH_TWO, :].reshape(P1, P2) * scale_two
    four_grad = total[:, HIGH_ONE + HIGH_TWO : PIECE_ROWS, :].reshape(P2, P2) * scale_one

    owned_sums = jnp.concatenate([cols.reshape(OWNED, P2), rows.reshape(OWNED, P1)], axis=1)
    sums = gather_owned(owned_sums, x_at, zh_at, core_at)
    return (
        input_grad,
        gating_grad,
        one_grad,
        mid[:, 0:P1],
        mid[:, P1 : 2 * P1],
        four_grad,
        sums[:, 0:P2] / math.sqrt(P1),
        sums[:, P2 : P1 + P2] / math.sqrt(P2),
    )


def solution(mesh):
    in_specs = (
        P("ch", "seq"),
        P("ch", "seq"),
        P("ch", "seq"),
        P(),
        P(),
        P(),
        P(),
        P("ch", None),
        P("ch", None),
    )
    out_specs = (P("ch", "seq"), P("ch", "seq"), P(), P(), P(), P(), P("ch", None), P("ch", None))
    return jax.shard_map(local, mesh=mesh, in_specs=in_specs, out_specs=out_specs, check_vma=False)
```

```python
import math

import jax
import jax.numpy as jnp
from jax import lax
from jax.experimental import pallas as pl
from jax.experimental.pallas import tpu as pltpu
from jax.sharding import PartitionSpec as P

P1 = 256
P2 = 512
C = 1536
N_SEQ = 16
N_CH = 8
N_CHIP = N_SEQ // 2
WIDTH = C // N_CH
OWNED = WIDTH // N_SEQ
ROWS = P1 // N_SEQ
LENGTH = ROWS * P2
LANES = P2 // 128
HEIGHT = LANES * ROWS
BLOCK = 96
STEPS = WIDTH // BLOCK
PIECES = 8
FINAL_BLOCK = 48
FORWARD_GROUP = 6
BACKWARD_GROUP = 3
SUM_ROWS = 2 * OWNED
HIGH_ONE = P2 // PIECES
HIGH_TWO = P1 // PIECES
PIECE_ROWS = 2 * HIGH_ONE + HIGH_TWO
AXES = ("seq", "ch")
MESSAGE_ORDER = (0, 2, 6, 3, 7, 1, 4, 5)

flt = jnp.float32
half = jnp.bfloat16


def params():
    return pltpu.CompilerParams(vmem_limit_bytes=63 * 1024 * 1024)


def cost(flops, moved):
    return pl.CostEstimate(flops=int(flops), bytes_accessed=int(moved), transcendentals=0)


def nn(a, b):
    return lax.dot_general(a, b, (((1,), (0,)), ((), ())), preferred_element_type=flt)


def nt(a, b):
    return lax.dot_general(a, b, (((1,), (1,)), ((), ())), preferred_element_type=flt)


def tn(a, b):
    return lax.dot_general(a, b, (((0,), (0,)), ((), ())), preferred_element_type=flt)


def to_slabs(mat, out_ref, index=()):
    for l in range(LANES):
        slab = mat[..., l * 128 : (l + 1) * 128]
        out_ref[(slice(None), *index, slice(l * ROWS, (l + 1) * ROWS))] = slab


def from_slabs(ref, index=()):
    slabs = [
        ref[(slice(None), *index, slice(l * ROWS, (l + 1) * ROWS))] for l in range(LANES)
    ]
    return jnp.concatenate(slabs, axis=-1)


def split_kernel(x_ref, out_ref):
    to_slabs(x_ref[...].reshape(BLOCK, ROWS, P2), out_ref)


def gate_kernel(g_ref, z_ref, keep_ref, send_ref):
    prod = (g_ref[...].astype(flt) * z_ref[...].astype(flt)).astype(half)
    mats = prod.reshape(BLOCK // (2 * OWNED), 2, OWNED, ROWS, P2)
    core = lax.axis_index("seq") % 2

    @pl.when(core == 0)
    def _():
        to_slabs(mats[:, 0], keep_ref, (slice(None),))
        to_slabs(mats[:, 1], send_ref, (slice(None),))

    @pl.when(core == 1)
    def _():
        to_slabs(mats[:, 1], keep_ref, (slice(None),))
        to_slabs(mats[:, 0], send_ref, (slice(None),))


def join_kernel(x_ref, out_ref):
    out_ref[...] = from_slabs(x_ref).reshape(BLOCK, LENGTH)


def final_kernel(h_ref, g_ref, four_ref, out_ref):
    for b in range(FINAL_BLOCK // 16):
        rows = slice(b * 16, b * 16 + 16)
        prod = nn(from_slabs(h_ref.at[rows]).reshape(16 * ROWS, P2), four_ref[...])
        prod = prod.reshape(16, LENGTH)
        out_ref[rows, :] = (g_ref[rows, :].astype(flt) * prod).astype(half)


def flat(n):
    return pl.BlockSpec((n, LENGTH), lambda i: (i, 0))


def mats(n):
    return pl.BlockSpec((n, HEIGHT, 128), lambda i: (i, 0, 0))


FLAT_SHAPE = jax.ShapeDtypeStruct((WIDTH, LENGTH), half)
MATS_SHAPE = jax.ShapeDtypeStruct((WIDTH, HEIGHT, 128), half)
SIZE = WIDTH * LENGTH * 2


def split(x):
    return pl.pallas_call(
        split_kernel, grid=(STEPS,), in_specs=[flat(BLOCK)], out_specs=mats(BLOCK), out_shape=MATS_SHAPE,
        compiler_params=params(), cost_estimate=cost(0, 2 * SIZE), name="split_rows",
    )(x)


def gate(g, z):
    spec = pl.BlockSpec((BLOCK // (2 * OWNED), OWNED, HEIGHT, 128), lambda i: (i, 0, 0, 0))
    shape = jax.ShapeDtypeStruct((N_CHIP, OWNED, HEIGHT, 128), half)
    return pl.pallas_call(
        gate_kernel, grid=(STEPS,), in_specs=[flat(BLOCK), flat(BLOCK)], out_specs=[spec, spec],
        out_shape=[shape, shape], compiler_params=params(), cost_estimate=cost(0, 3 * SIZE),
        name="gate_rows",
    )(g, z)


def join(x):
    return pl.pallas_call(
        join_kernel, grid=(STEPS,), in_specs=[mats(BLOCK)], out_specs=flat(BLOCK), out_shape=FLAT_SHAPE,
        compiler_params=params(), cost_estimate=cost(0, 2 * SIZE), name="join_rows",
    )(x)


def final(h, g, four):
    return pl.pallas_call(
        final_kernel, grid=(WIDTH // FINAL_BLOCK,),
        in_specs=[mats(FINAL_BLOCK), flat(FINAL_BLOCK), pl.BlockSpec((P2, P2), lambda i: (0, 0))],
        out_specs=flat(FINAL_BLOCK), out_shape=FLAT_SHAPE, compiler_params=params(),
        cost_estimate=cost(2 * WIDTH * LENGTH * P2, 3 * SIZE), name="final_rows",
    )(h, g, four)


def forward_kernel(x_ref, one_ref, two_ref, three_ref, kc_ref, kr_ref, h_ref):
    for q in range(FORWARD_GROUP):
        x = from_slabs(x_ref, (q,)).reshape(P1, P2)
        first = (nn(x, one_ref[...]) * kc_ref[q]).astype(half)
        left = (nn(two_ref[...], first) * kr_ref[q]).astype(half)
        second = nn(three_ref[...], left).astype(half)
        to_slabs(second.reshape(N_SEQ, ROWS, P2), h_ref, (q,))


def backward_channels(e_ref, refs, accs, dx_ref, sums_ref):
    x_ref, one_ref, two_ref, three_ref, four_ref, two_t_ref, three_t_ref, kc_ref, kr_ref = refs
    acc_one, acc_two, acc_three, acc_four = accs
    step = pl.program_id(0)
    for q in range(BACKWARD_GROUP):
        kc = kc_ref[q]
        kr = kr_ref[q]
        x = from_slabs(x_ref, (q,)).reshape(P1, P2)
        e = from_slabs(e_ref, (q,)).reshape(P1, P2)
        first_prod = nn(x, one_ref[...])
        first = (first_prod * kc).astype(half)
        left_prod = nn(two_ref[...], first)
        left = (left_prod * kr).astype(half)
        second = nn(three_ref[...], left).astype(half)
        d_second = nt(e, four_ref[...]).astype(half)
        d_left = nn(three_t_ref[...], d_second)
        row_terms = d_left * left_prod
        row_terms = sum(row_terms[:, l * 128 : (l + 1) * 128] for l in range(LANES))
        row_sums = jnp.sum(row_terms.T, axis=0, keepdims=True)
        d_prod = (d_left * kr).astype(half)
        d_first = nn(two_t_ref[...], d_prod).astype(half).astype(flt)
        col_sums = jnp.sum(d_first * first_prod, axis=0, keepdims=True)
        d_inner = (d_first * kc).astype(half)
        d_x = nt(d_inner, one_ref[...]).astype(half)
        to_slabs(d_x.reshape(N_SEQ, ROWS, P2), dx_ref, (q,))
        channel = step * BACKWARD_GROUP + q
        sums_ref[pl.ds(channel, 1), :] = col_sums
        sums_ref[pl.ds(OWNED + channel, 1), 0:P1] = row_sums
        acc_four[...] += tn(second, e)
        acc_three[...] += nt(d_second, left)
        acc_two[...] += nt(d_prod, first)
        acc_one[...] += tn(x, d_inner)


def backward_kernel(*refs):
    e_parts = refs[9 : 9 + N_CHIP]
    dx_ref, sums_ref, keep_ref, send_ref, *accs, e_ref = refs[9 + N_CHIP :]
    step = pl.program_id(0)
    seq = lax.axis_index("seq")
    for offset, ref in zip(MESSAGE_ORDER, e_parts):
        source = seq ^ (2 * offset)
        e_ref[source] = ref[0]
        e_ref[source ^ 1] = ref[1]

    @pl.when(step == 0)
    def _():
        for ref in (*accs, sums_ref):
            ref[...] = jnp.zeros_like(ref)

    backward_channels(e_ref, refs[:9], accs, dx_ref, sums_ref)
    core = seq % 2
    acc_one, acc_two, acc_three, acc_four = accs

    def write(out_ref, first_piece):
        for p in range(PIECES // 2):
            at = first_piece + p
            wide = slice(at * HIGH_ONE, (at + 1) * HIGH_ONE)
            tall = slice(at * HIGH_TWO, (at + 1) * HIGH_TWO)
            middle = slice(HIGH_ONE, HIGH_ONE + HIGH_TWO)
            dtype = out_ref.dtype
            out_ref[p, 0:HIGH_ONE, :] = acc_one[wide, :].astype(dtype)
            out_ref[p, middle, 0:P1] = acc_two[tall, :].astype(dtype)
            out_ref[p, middle, P1 : 2 * P1] = acc_three[tall, :].astype(dtype)
            out_ref[p, HIGH_ONE + HIGH_TWO : PIECE_ROWS, :] = acc_four[wide, :].astype(dtype)

    for c in range(2):

        @pl.when((step == OWNED // BACKWARD_GROUP - 1) & (core == c))
        def _(c=c):
            write(keep_ref, c * (PIECES // 2))
            write(send_ref, (1 - c) * (PIECES // 2))


def whole(*shape):
    return pl.BlockSpec(shape, lambda q: (0,) * len(shape))


def own(n):
    return pl.BlockSpec((N_SEQ, n, HEIGHT, 128), lambda q: (0, q, 0, 0))


def col(n):
    return pl.BlockSpec((n, 1, P2), lambda q: (q, 0, 0))


def row(n):
    return pl.BlockSpec((n, P1, 1), lambda q: (q, 0, 0))


OWN_SHAPE = jax.ShapeDtypeStruct((N_SEQ, OWNED, HEIGHT, 128), half)
BIG = 2 * P1 * P2 * P2 * OWNED
SMALL = 2 * P1 * P1 * P2 * OWNED


def forward(x, one, two, three, kc, kr):
    n = FORWARD_GROUP
    return pl.pallas_call(
        forward_kernel, grid=(OWNED // n,),
        in_specs=[own(n), whole(P2, P2), whole(P1, P1), whole(P1, P1), col(n), row(n)],
        out_specs=own(n), out_shape=OWN_SHAPE, compiler_params=params(),
        cost_estimate=cost(BIG + 2 * SMALL, 2 * SIZE), name="forward_owned",
    )(x, one, two, three, kc, kr)


ACC_SHAPES = [(P2, P2), (P1, P1), (P1, P1), (P2, P2)]


def backward(args, e_parts):
    n = BACKWARD_GROUP
    piece = (PIECES // 2, PIECE_ROWS, P2)
    return pl.pallas_call(
        backward_kernel, grid=(OWNED // n,),
        in_specs=[
            own(n), whole(P2, P2), whole(P1, P1), whole(P1, P1), whole(P2, P2),
            whole(P1, P1), whole(P1, P1), col(n), row(n),
        ]
        + [pl.BlockSpec((2, n, HEIGHT, 128), lambda q: (0, q, 0, 0))] * N_CHIP,
        out_specs=[own(n), whole(SUM_ROWS, P2), whole(*piece), whole(*piece)],
        out_shape=[
            OWN_SHAPE, jax.ShapeDtypeStruct((SUM_ROWS, P2), flt),
            jax.ShapeDtypeStruct(piece, flt), jax.ShapeDtypeStruct(piece, half),
        ],
        scratch_shapes=[
            *(pltpu.VMEM(s, flt) for s in ACC_SHAPES),
            pltpu.VMEM((N_SEQ, n, HEIGHT, 128), half),
        ],
        compiler_params=params(),
        cost_estimate=cost(5 * BIG + 6 * SMALL, 3 * SIZE), name="backward_owned",
    )(*args, *e_parts)


def swap_pairs(x=0, zh=0, core=0, zl=0, y=0):
    flip_seq = x * 4 + zh * 2 + core
    flip_ch = zl * 4 + y
    return [
        (s * N_CH + c, (s ^ flip_seq) * N_CH + (c ^ flip_ch))
        for s in range(N_SEQ)
        for c in range(N_CH)
    ]


def swap(v, **flips):
    return lax.ppermute(v, AXES, swap_pairs(**flips))


def pick(v, index):
    return lax.dynamic_index_in_dim(v, index, 0, keepdims=False)


def in_order(bit, mine, theirs):
    return jnp.where(bit == 0, jnp.stack([mine, theirs]), jnp.stack([theirs, mine]))


def four_in_order(place, own, near, far, other):
    low = in_order(place & 1, own, near)
    high = in_order(place & 1, far, other)
    return in_order(place >> 1, low, high).reshape(4, *own.shape)


def sum_over_four(v, axes, extra, extra_axes):
    v = v.astype(half)
    got = []
    held = []
    for flips in axes:
        if flips in extra_axes:
            both = swap(jnp.concatenate([v, extra]), **flips)
            got.append(both[:PIECE_ROWS])
            held.append(both[PIECE_ROWS:])
        else:
            got.append(swap(v, **flips))
    one, two, three = got
    return (v.astype(flt) + one.astype(flt)) + (two.astype(flt) + three.astype(flt)), held


def reduce_grads(keep, send, y):
    kept = keep + swap(send, core=1).astype(flt)
    got = [swap(pick(kept, y ^ d).astype(half), y=d).astype(flt) for d in (1, 2, 3)]
    return pick(kept, y) + got[0] + got[1] + got[2]


def gather_grads(mine, core, y):
    near, far, other = (swap(mine, y=d) for d in (1, 2, 3))
    mine = four_in_order(y, mine, near, far, other)
    both = in_order(core, mine, swap(mine, core=1))
    return both.reshape(PIECES, PIECE_ROWS, P2)


def after(*values):
    return lax.optimization_barrier(values)


def exchange(v):
    rows = v.reshape(-1, 128)
    return lax.all_to_all(rows, "seq", split_axis=0, concat_axis=0, tiled=True)


def exchange_by_chip(keep, send, chip):
    sibling = swap(send, core=1)
    parts = []
    for offset in MESSAGE_ORDER:
        message = jnp.stack([pick(keep, chip ^ offset), pick(sibling, chip ^ offset)])
        if offset:
            message = swap(message, x=offset >> 1, zh=offset & 1)
        parts.append(message)
    return parts


def local(
    inputs,
    gating,
    upstream,
    factor_one,
    factor_two,
    factor_three,
    factor_four,
    kernel_cols,
    kernel_rows,
):
    seq = lax.axis_index("seq")
    ch = lax.axis_index("ch")
    x_at, zh_at, core_at, y_at = seq >> 2, (seq >> 1) & 1, seq & 1, ch & 3
    owned = (N_SEQ, OWNED, HEIGHT, 128)
    by_channel = (WIDTH, HEIGHT, 128)
    kc = lax.dynamic_slice_in_dim(kernel_cols, seq * OWNED, OWNED, 0).reshape(OWNED, 1, P2)
    kr = lax.dynamic_slice_in_dim(kernel_rows, seq * OWNED, OWNED, 0).reshape(OWNED, P1, 1)

    x_own = exchange(split(inputs)).reshape(owned)
    e_parts = exchange_by_chip(*gate(upstream, gating), seq >> 1)
    h_own = forward(x_own, factor_one, factor_two, factor_three, kc, kr)
    h_own, *e_parts = after(h_own, *e_parts)
    h_rows = exchange(h_own).reshape(by_channel)
    args = (
        x_own, factor_one, factor_two, factor_three, factor_four, factor_two.T, factor_three.T,
        kc, kr,
    )
    dx_own, sums, keep, send = backward(args, e_parts)
    sums = sums.astype(half)
    sums = in_order(core_at, sums, swap(sums, core=1)).reshape(2 * SUM_ROWS, P2)
    mine = reduce_grads(keep, send, y_at)
    mine, sums, h_rows = after(mine, sums, h_rows)
    over_x = [dict(x=1), dict(x=2), dict(x=3)]
    mine, held = sum_over_four(mine, over_x, sums, over_x)
    sums = four_in_order(x_at, sums, *held).reshape(8 * SUM_ROWS, P2)
    over_z = [dict(zl=1), dict(zh=1), dict(zh=1, zl=1)]
    mine, held = sum_over_four(mine, over_z, sums, over_z[1:2])
    sums = in_order(zh_at, sums, held[0]).reshape(2, 4, 2, SUM_ROWS, P2)
    mine, sums, dx_own = after(mine.astype(half), sums, dx_own)
    dx_rows = exchange(dx_own).reshape(by_channel)
    sums = sums.swapaxes(0, 1).reshape(N_SEQ, SUM_ROWS, P2).astype(flt)
    cols = sums[:, 0:OWNED].reshape(WIDTH, P2)
    rows = sums[:, OWNED : 2 * OWNED, 0:P1].reshape(WIDTH, P1)
    total = gather_grads(mine, core_at, y_at)
    gating_grad = final(h_rows, upstream, factor_four)
    total = total.astype(flt)
    scale_one = 1.0 / math.sqrt(P1 * C)
    scale_two = 1.0 / math.sqrt(P2 * C)
    one_grad = total[:, 0:HIGH_ONE, :].reshape(P2, P2) * scale_one
    mid = total[:, HIGH_ONE : HIGH_ONE + HIGH_TWO, :].reshape(P1, P2) * scale_two
    four_grad = total[:, HIGH_ONE + HIGH_TWO : PIECE_ROWS, :].reshape(P2, P2) * scale_one
    small = (
        gating_grad,
        one_grad,
        mid[:, 0:P1],
        mid[:, P1 : 2 * P1],
        four_grad,
        cols * (1.0 / math.sqrt(P1)),
        rows * (1.0 / math.sqrt(P2)),
    )
    dx_rows, *small = after(dx_rows, *small)
    return join(dx_rows), *small


def solution(mesh):
    in_specs = (
        P("ch", "seq"),
        P("ch", "seq"),
        P("ch", "seq"),
        P(),
        P(),
        P(),
        P(),
        P("ch", None),
        P("ch", None),
    )
    out_specs = (P("ch", "seq"), P("ch", "seq"), P(), P(), P(), P(), P("ch", None), P("ch", None))
    return jax.shard_map(local, mesh=mesh, in_specs=in_specs, out_specs=out_specs, check_vma=False)
```

```python
import math

import jax
import jax.numpy as jnp
from jax import lax
from jax.experimental import pallas as pl
from jax.experimental.pallas import tpu as pltpu
from jax.sharding import PartitionSpec as P

P1 = 256
P2 = 512
C = 1536
N_SEQ = 16
N_CH = 8
N_CHIP = N_SEQ // 2
WIDTH = C // N_CH
OWNED = WIDTH // N_SEQ
ROWS = P1 // N_SEQ
LENGTH = ROWS * P2
LANES = P2 // 128
HEIGHT = LANES * ROWS
BLOCK = 96
STEPS = WIDTH // BLOCK
PIECES = 8
FINAL_BLOCK = 48
FORWARD_GROUP = 3
BACKWARD_GROUP = 3
SUM_ROWS = 2 * OWNED
HIGH_ONE = P2 // PIECES
HIGH_TWO = P1 // PIECES
PIECE_ROWS = 2 * HIGH_ONE + HIGH_TWO
AXES = ("seq", "ch")
MESSAGE_ORDER = (0, 2, 6, 3, 7, 1, 4, 5)

flt = jnp.float32
half = jnp.bfloat16


def params():
    return pltpu.CompilerParams(vmem_limit_bytes=63 * 1024 * 1024)


def cost(flops, moved):
    return pl.CostEstimate(flops=int(flops), bytes_accessed=int(moved), transcendentals=0)


def nn(a, b):
    return lax.dot_general(a, b, (((1,), (0,)), ((), ())), preferred_element_type=flt)


def nt(a, b):
    return lax.dot_general(a, b, (((1,), (1,)), ((), ())), preferred_element_type=flt)


def tn(a, b):
    return lax.dot_general(a, b, (((0,), (0,)), ((), ())), preferred_element_type=flt)


def to_slabs(mat, out_ref, index=()):
    for l in range(LANES):
        slab = mat[..., l * 128 : (l + 1) * 128]
        out_ref[(slice(None), *index, slice(l * ROWS, (l + 1) * ROWS))] = slab


def from_slabs(ref, index=()):
    slabs = [
        ref[(slice(None), *index, slice(l * ROWS, (l + 1) * ROWS))] for l in range(LANES)
    ]
    return jnp.concatenate(slabs, axis=-1)


def split_kernel(x_ref, out_ref):
    to_slabs(x_ref[...].reshape(BLOCK, ROWS, P2), out_ref)


def gate_kernel(g_ref, z_ref, keep_ref, send_ref):
    prod = (g_ref[...].astype(flt) * z_ref[...].astype(flt)).astype(half)
    mats = prod.reshape(BLOCK // (2 * OWNED), 2, OWNED, ROWS, P2)
    core = lax.axis_index("seq") % 2

    @pl.when(core == 0)
    def _():
        to_slabs(mats[:, 0], keep_ref, (slice(None),))
        to_slabs(mats[:, 1], send_ref, (slice(None),))

    @pl.when(core == 1)
    def _():
        to_slabs(mats[:, 1], keep_ref, (slice(None),))
        to_slabs(mats[:, 0], send_ref, (slice(None),))


def join_kernel(x_ref, out_ref):
    out_ref[...] = from_slabs(x_ref).reshape(BLOCK, LENGTH)


def final_kernel(h_ref, g_ref, four_ref, out_ref):
    for b in range(FINAL_BLOCK // 16):
        rows = slice(b * 16, b * 16 + 16)
        prod = nn(from_slabs(h_ref.at[rows]).reshape(16 * ROWS, P2), four_ref[...])
        prod = prod.reshape(16, LENGTH)
        out_ref[rows, :] = (g_ref[rows, :].astype(flt) * prod).astype(half)


def flat(n):
    return pl.BlockSpec((n, LENGTH), lambda i: (i, 0))


def mats(n):
    return pl.BlockSpec((n, HEIGHT, 128), lambda i: (i, 0, 0))


FLAT_SHAPE = jax.ShapeDtypeStruct((WIDTH, LENGTH), half)
MATS_SHAPE = jax.ShapeDtypeStruct((WIDTH, HEIGHT, 128), half)
SIZE = WIDTH * LENGTH * 2


def split(x):
    return pl.pallas_call(
        split_kernel, grid=(STEPS,), in_specs=[flat(BLOCK)], out_specs=mats(BLOCK), out_shape=MATS_SHAPE,
        compiler_params=params(), cost_estimate=cost(0, 2 * SIZE), name="split_rows",
    )(x)


def gate(g, z):
    spec = pl.BlockSpec((BLOCK // (2 * OWNED), OWNED, HEIGHT, 128), lambda i: (i, 0, 0, 0))
    shape = jax.ShapeDtypeStruct((N_CHIP, OWNED, HEIGHT, 128), half)
    return pl.pallas_call(
        gate_kernel, grid=(STEPS,), in_specs=[flat(BLOCK), flat(BLOCK)], out_specs=[spec, spec],
        out_shape=[shape, shape], compiler_params=params(), cost_estimate=cost(0, 3 * SIZE),
        name="gate_rows",
    )(g, z)


def join(x):
    return pl.pallas_call(
        join_kernel, grid=(STEPS,), in_specs=[mats(BLOCK)], out_specs=flat(BLOCK), out_shape=FLAT_SHAPE,
        compiler_params=params(), cost_estimate=cost(0, 2 * SIZE), name="join_rows",
    )(x)


def final(h, g, four):
    return pl.pallas_call(
        final_kernel, grid=(WIDTH // FINAL_BLOCK,),
        in_specs=[mats(FINAL_BLOCK), flat(FINAL_BLOCK), pl.BlockSpec((P2, P2), lambda i: (0, 0))],
        out_specs=flat(FINAL_BLOCK), out_shape=FLAT_SHAPE, compiler_params=params(),
        cost_estimate=cost(2 * WIDTH * LENGTH * P2, 3 * SIZE), name="final_rows",
    )(h, g, four)


def forward_kernel(
    x_ref, one_ref, two_ref, three_ref, kc_ref, kr_ref, h_ref, first_ref, left_ref
):
    for q in range(FORWARD_GROUP):
        x = from_slabs(x_ref, (q,)).reshape(P1, P2)
        first_prod = nn(x, one_ref[...])
        first_ref[q] = first_prod
        first = (first_prod * kc_ref[q]).astype(half)
        left_prod = nn(two_ref[...], first)
        left_ref[q] = left_prod
        left = (left_prod * kr_ref[q]).astype(half)
        second = nn(three_ref[...], left).astype(half)
        to_slabs(second.reshape(N_SEQ, ROWS, P2), h_ref, (q,))


def backward_channels(e_ref, refs, accs, dx_ref, sums_ref):
    x_ref, h_ref, first_ref, left_ref, one_ref, four_ref, two_t_ref, three_t_ref = refs[:8]
    kc_ref, kr_ref = refs[8:]
    acc_one, acc_two, acc_three, acc_four = accs
    step = pl.program_id(0)
    for q in range(BACKWARD_GROUP):
        kc = kc_ref[q]
        kr = kr_ref[q]
        x = from_slabs(x_ref, (q,)).reshape(P1, P2)
        e = from_slabs(e_ref, (q,)).reshape(P1, P2)
        second = from_slabs(h_ref, (q,)).reshape(P1, P2)
        first_prod = first_ref[q]
        first = (first_prod * kc).astype(half)
        left_prod = left_ref[q]
        left = (left_prod * kr).astype(half)
        d_second = nt(e, four_ref[...]).astype(half)
        d_left = nn(three_t_ref[...], d_second)
        row_terms = d_left * left_prod
        row_terms = sum(row_terms[:, l * 128 : (l + 1) * 128] for l in range(LANES))
        row_sums = jnp.sum(row_terms.T, axis=0, keepdims=True)
        d_prod = (d_left * kr).astype(half)
        d_first = nn(two_t_ref[...], d_prod).astype(half).astype(flt)
        col_sums = jnp.sum(d_first * first_prod, axis=0, keepdims=True)
        d_inner = (d_first * kc).astype(half)
        d_x = nt(d_inner, one_ref[...]).astype(half)
        to_slabs(d_x.reshape(N_SEQ, ROWS, P2), dx_ref, (q,))
        channel = step * BACKWARD_GROUP + q
        sums_ref[pl.ds(channel, 1), :] = col_sums
        sums_ref[pl.ds(OWNED + channel, 1), 0:P1] = row_sums
        acc_four[...] += tn(second, e)
        acc_three[...] += nt(d_second, left)
        acc_two[...] += nt(d_prod, first)
        acc_one[...] += tn(x, d_inner)


def backward_kernel(*refs):
    e_parts = refs[10 : 10 + N_CHIP]
    dx_ref, sums_ref, keep_ref, send_ref, *accs, e_ref = refs[10 + N_CHIP :]
    step = pl.program_id(0)
    seq = lax.axis_index("seq")
    for offset, ref in zip(MESSAGE_ORDER, e_parts):
        source = seq ^ (2 * offset)
        e_ref[source] = ref[0]
        e_ref[source ^ 1] = ref[1]

    @pl.when(step == 0)
    def _():
        for ref in (*accs, sums_ref):
            ref[...] = jnp.zeros_like(ref)

    backward_channels(e_ref, refs[:10], accs, dx_ref, sums_ref)
    core = seq % 2
    acc_one, acc_two, acc_three, acc_four = accs

    def write(out_ref, first_piece):
        for p in range(PIECES // 2):
            at = first_piece + p
            wide = slice(at * HIGH_ONE, (at + 1) * HIGH_ONE)
            tall = slice(at * HIGH_TWO, (at + 1) * HIGH_TWO)
            middle = slice(HIGH_ONE, HIGH_ONE + HIGH_TWO)
            dtype = out_ref.dtype
            out_ref[p, 0:HIGH_ONE, :] = acc_one[wide, :].astype(dtype)
            out_ref[p, middle, 0:P1] = acc_two[tall, :].astype(dtype)
            out_ref[p, middle, P1 : 2 * P1] = acc_three[tall, :].astype(dtype)
            out_ref[p, HIGH_ONE + HIGH_TWO : PIECE_ROWS, :] = acc_four[wide, :].astype(dtype)

    for c in range(2):

        @pl.when((step == OWNED // BACKWARD_GROUP - 1) & (core == c))
        def _(c=c):
            write(keep_ref, c * (PIECES // 2))
            write(send_ref, (1 - c) * (PIECES // 2))


def whole(*shape):
    return pl.BlockSpec(shape, lambda q: (0,) * len(shape))


def own(n):
    return pl.BlockSpec((N_SEQ, n, HEIGHT, 128), lambda q: (0, q, 0, 0))


def mat(n):
    return pl.BlockSpec((n, P1, P2), lambda q: (q, 0, 0))


def col(n):
    return pl.BlockSpec((n, 1, P2), lambda q: (q, 0, 0))


def row(n):
    return pl.BlockSpec((n, P1, 1), lambda q: (q, 0, 0))


OWN_SHAPE = jax.ShapeDtypeStruct((N_SEQ, OWNED, HEIGHT, 128), half)
MAT_SHAPE = jax.ShapeDtypeStruct((OWNED, P1, P2), flt)
BIG = 2 * P1 * P2 * P2 * OWNED
SMALL = 2 * P1 * P1 * P2 * OWNED


def forward(x, one, two, three, kc, kr):
    n = FORWARD_GROUP
    return pl.pallas_call(
        forward_kernel, grid=(OWNED // n,),
        in_specs=[own(n), whole(P2, P2), whole(P1, P1), whole(P1, P1), col(n), row(n)],
        out_specs=[own(n), mat(n), mat(n)], out_shape=[OWN_SHAPE, MAT_SHAPE, MAT_SHAPE],
        compiler_params=params(), cost_estimate=cost(BIG + 2 * SMALL, 6 * SIZE),
        name="forward_owned",
    )(x, one, two, three, kc, kr)


ACC_SHAPES = [(P2, P2), (P1, P1), (P1, P1), (P2, P2)]


def backward(args, e_parts):
    n = BACKWARD_GROUP
    piece = (PIECES // 2, PIECE_ROWS, P2)
    return pl.pallas_call(
        backward_kernel, grid=(OWNED // n,),
        in_specs=[
            own(n), own(n), mat(n), mat(n), whole(P2, P2), whole(P2, P2),
            whole(P1, P1), whole(P1, P1), col(n), row(n),
        ]
        + [pl.BlockSpec((2, n, HEIGHT, 128), lambda q: (0, q, 0, 0))] * N_CHIP,
        out_specs=[own(n), whole(SUM_ROWS, P2), whole(*piece), whole(*piece)],
        out_shape=[
            OWN_SHAPE, jax.ShapeDtypeStruct((SUM_ROWS, P2), flt),
            jax.ShapeDtypeStruct(piece, flt), jax.ShapeDtypeStruct(piece, half),
        ],
        scratch_shapes=[
            *(pltpu.VMEM(s, flt) for s in ACC_SHAPES),
            pltpu.VMEM((N_SEQ, n, HEIGHT, 128), half),
        ],
        compiler_params=params(),
        cost_estimate=cost(4 * BIG + 4 * SMALL, 8 * SIZE), name="backward_owned",
    )(*args, *e_parts)


def swap_pairs(x=0, zh=0, core=0, zl=0, y=0):
    flip_seq = x * 4 + zh * 2 + core
    flip_ch = zl * 4 + y
    return [
        (s * N_CH + c, (s ^ flip_seq) * N_CH + (c ^ flip_ch))
        for s in range(N_SEQ)
        for c in range(N_CH)
    ]


def swap(v, **flips):
    return lax.ppermute(v, AXES, swap_pairs(**flips))


def pick(v, index):
    return lax.dynamic_index_in_dim(v, index, 0, keepdims=False)


def in_order(bit, mine, theirs):
    return jnp.where(bit == 0, jnp.stack([mine, theirs]), jnp.stack([theirs, mine]))


def four_in_order(place, own, near, far, other):
    low = in_order(place & 1, own, near)
    high = in_order(place & 1, far, other)
    return in_order(place >> 1, low, high).reshape(4, *own.shape)


def sum_over_four(v, axes, extra, extra_axes):
    v = v.astype(half)
    got = []
    held = []
    for flips in axes:
        if flips in extra_axes:
            both = swap(jnp.concatenate([v, extra]), **flips)
            got.append(both[:PIECE_ROWS])
            held.append(both[PIECE_ROWS:])
        else:
            got.append(swap(v, **flips))
    one, two, three = got
    return (v.astype(flt) + one.astype(flt)) + (two.astype(flt) + three.astype(flt)), held


def reduce_grads(keep, send, y):
    kept = keep + swap(send, core=1).astype(flt)
    got = [swap(pick(kept, y ^ d).astype(half), y=d).astype(flt) for d in (1, 2, 3)]
    return pick(kept, y) + got[0] + got[1] + got[2]


def gather_grads(mine, core, y):
    near, far, other = (swap(mine, y=d) for d in (1, 2, 3))
    mine = four_in_order(y, mine, near, far, other)
    both = in_order(core, mine, swap(mine, core=1))
    return both.reshape(PIECES, PIECE_ROWS, P2)


def after(*values):
    return lax.optimization_barrier(values)


def exchange(v):
    rows = v.reshape(-1, 128)
    return lax.all_to_all(rows, "seq", split_axis=0, concat_axis=0, tiled=True)


def exchange_by_chip(keep, send, chip):
    sibling = swap(send, core=1)
    parts = []
    for offset in MESSAGE_ORDER:
        message = jnp.stack([pick(keep, chip ^ offset), pick(sibling, chip ^ offset)])
        if offset:
            message = swap(message, x=offset >> 1, zh=offset & 1)
        parts.append(message)
    return parts


def local(
    inputs,
    gating,
    upstream,
    factor_one,
    factor_two,
    factor_three,
    factor_four,
    kernel_cols,
    kernel_rows,
):
    seq = lax.axis_index("seq")
    ch = lax.axis_index("ch")
    x_at, zh_at, core_at, y_at = seq >> 2, (seq >> 1) & 1, seq & 1, ch & 3
    owned = (N_SEQ, OWNED, HEIGHT, 128)
    by_channel = (WIDTH, HEIGHT, 128)
    kc = lax.dynamic_slice_in_dim(kernel_cols, seq * OWNED, OWNED, 0).reshape(OWNED, 1, P2)
    kr = lax.dynamic_slice_in_dim(kernel_rows, seq * OWNED, OWNED, 0).reshape(OWNED, P1, 1)

    x_own = exchange(split(inputs)).reshape(owned)
    e_parts = exchange_by_chip(*gate(upstream, gating), seq >> 1)
    h_own, first, left = forward(x_own, factor_one, factor_two, factor_three, kc, kr)
    *arrived, last = e_parts
    h_own, two_t, three_t, *arrived = after(h_own, factor_two.T, factor_three.T, *arrived)
    h_rows = exchange(h_own).reshape(by_channel)
    args = (x_own, h_own, first, left, factor_one, factor_four, two_t, three_t, kc, kr)
    dx_own, sums, keep, send = backward(args, (*arrived, last))
    sums = sums.astype(half)
    sums = in_order(core_at, sums, swap(sums, core=1)).reshape(2 * SUM_ROWS, P2)
    mine = reduce_grads(keep, send, y_at)
    mine, sums, h_rows = after(mine, sums, h_rows)
    over_x = [dict(x=1), dict(x=2), dict(x=3)]
    mine, held = sum_over_four(mine, over_x, sums, over_x)
    sums = four_in_order(x_at, sums, *held).reshape(8 * SUM_ROWS, P2)
    over_z = [dict(zl=1), dict(zh=1), dict(zh=1, zl=1)]
    mine, held = sum_over_four(mine, over_z, sums, over_z[1:2])
    sums = in_order(zh_at, sums, held[0]).reshape(2, 4, 2, SUM_ROWS, P2)
    mine, sums, dx_own = after(mine.astype(half), sums, dx_own)
    dx_rows = exchange(dx_own).reshape(by_channel)
    sums = sums.swapaxes(0, 1).reshape(N_SEQ, SUM_ROWS, P2).astype(flt)
    cols = sums[:, 0:OWNED].reshape(WIDTH, P2)
    rows = sums[:, OWNED : 2 * OWNED, 0:P1].reshape(WIDTH, P1)
    total = gather_grads(mine, core_at, y_at)
    gating_grad = final(h_rows, upstream, factor_four)
    total = total.astype(flt)
    scale_one = 1.0 / math.sqrt(P1 * C)
    scale_two = 1.0 / math.sqrt(P2 * C)
    one_grad = total[:, 0:HIGH_ONE, :].reshape(P2, P2) * scale_one
    mid = total[:, HIGH_ONE : HIGH_ONE + HIGH_TWO, :].reshape(P1, P2) * scale_two
    four_grad = total[:, HIGH_ONE + HIGH_TWO : PIECE_ROWS, :].reshape(P2, P2) * scale_one
    small = (
        gating_grad,
        one_grad,
        mid[:, 0:P1],
        mid[:, P1 : 2 * P1],
        four_grad,
        cols * (1.0 / math.sqrt(P1)),
        rows * (1.0 / math.sqrt(P2)),
    )
    dx_rows, *small = after(dx_rows, *small)
    return join(dx_rows), *small


def solution(mesh):
    in_specs = (
        P("ch", "seq"),
        P("ch", "seq"),
        P("ch", "seq"),
        P(),
        P(),
        P(),
        P(),
        P("ch", None),
        P("ch", None),
    )
    out_specs = (P("ch", "seq"), P("ch", "seq"), P(), P(), P(), P(), P("ch", None), P("ch", None))
    return jax.shard_map(local, mesh=mesh, in_specs=in_specs, out_specs=out_specs, check_vma=False)
```
